512 devices in a mesh: rep: 32 (over x, y, z_hi), fsdp: 16 (over z_lo, core).
Axes of the slice: x: 4, y: 4, z: 16 (z_hi: 2, z_lo: 8; z = z_hi * 8 + z_lo), core: 2. Of those that a mesh axis runs over, the one named last changes fastest.
Arguments:
- activations: bfloat16 [65536, 8192], P(('rep', 'fsdp')), may hold values from -6 to 6
- key_grads: bfloat16 [65536, 512], P(('rep', 'fsdp')), may hold values from -6 to 6
- params: float32 [32, 8192, 512], P('rep', 'fsdp'), may hold values from -6 to 6
- first_moment: bfloat16 [32, 8192, 512], P('rep', 'fsdp'), may hold values from -4 to 4
- second_moment: bfloat16 [32, 8192, 512], P('rep', 'fsdp'), may hold values from 0.0099487305 to 1
- step_index: int32 [1], replicated, may hold values from 0 to 63
Outputs:
- key_out: bfloat16 [65536, 512], P(('rep', 'fsdp'))
- averaged: bfloat16 [32, 8192, 512], P('rep', 'fsdp')
The draws below stay inside these ranges and needn't reach their ends.
All inputs are finite; a program needn't handle non-finite values.
Results may differ from the reference program's by a relative error of at most 0.0049.
Values may be sent and summed in bfloat16 or wider, within the bound.
A program may use at most 64 MiB of HBM per device.

```python
import math
import jax
import jax.numpy as jnp
from jax import lax

D = 8192
KVW = 512
TOK_DEV = 128
REPLICAS = 32
TOKENS = 65536
N_REP = 32
N_FSDP = 16


def steps_of(rng, extent, shards, smallest, high):
    level = 1.0
    for axis_at, parts in shards:
        draws = jax.random.uniform(jax.random.fold_in(jax.random.fold_in(rng, 6), axis_at), (parts,), jnp.float32, smallest / len(shards), high / len(shards))
        level = level * jnp.repeat(jnp.exp(draws), extent[axis_at] // parts).reshape((-1,) + (1,) * (len(extent) - 1 - axis_at))
    return level


def centred(key, extent, width, most, cuts=(), kind=jnp.bfloat16):
    entries = width * jax.random.normal(key, extent, jnp.float32)
    if cuts:
        entries = entries * steps_of(key, extent, cuts, -0.22, 0.18)
    return jnp.clip(entries, -most, most).astype(kind)


def setup_inputs(seed: int = 0) -> dict:
    seeds = jax.random.split(jax.random.key(seed), 7)
    activations = centred(seeds[0], (TOKENS, D), 1.0, 6.0, ((0, 512),))
    key_grads = centred(seeds[1], (TOKENS, KVW), 1.0, 6.0, ((0, 512),))
    params = centred(seeds[2], (REPLICAS, D, KVW), 1.0, 6.0, ((0, 32), (1, 16)), jnp.float32)
    first_moment = centred(seeds[3], (REPLICAS, D, KVW), 0.3, 4.0, ((0, 32), (1, 16)))
    second_moment = jnp.clip(jnp.exp(math.log(1.0) - 4.61031033 * jax.random.uniform(seeds[4], (REPLICAS, D, KVW), jnp.float32) ** steps_of(seeds[4], (REPLICAS, D, KVW), ((0, 32), (1, 16)), -0.2, 0.2)), 0.0099487305, 1.0).astype(jnp.bfloat16)
    step_index = jax.random.randint(seeds[5], (1,), 0, 64).astype(jnp.int32)
    return {"activations": activations, "key_grads": key_grads, "params": params, "first_moment": first_moment, "second_moment": second_moment, "step_index": step_index}


beta_one = 0.9
beta_two = 0.95
learn_rate = 0.25
epsilon = 1e-08

def adam_step(params, first_moment, second_moment, gradient, step_index):
    steps = (step_index[0] + 1).astype(jnp.float32)
    moment_one = beta_one * first_moment.astype(jnp.float32) + (1.0 - beta_one) * gradient
    moment_two = beta_two * second_moment.astype(jnp.float32) + (1.0 - beta_two) * gradient * gradient
    corr_one = 1.0 - jnp.power(jnp.float32(beta_one), steps)
    corr_two = 1.0 - jnp.power(jnp.float32(beta_two), steps)
    return params - learn_rate * (moment_one / corr_one) / (jnp.sqrt(moment_two / corr_two) + epsilon)

def reference(activations, key_grads, params, first_moment, second_moment, step_index):
    factor = D ** (-0.5)
    row_count = TOK_DEV * N_FSDP
    inputs = activations.reshape(REPLICAS, row_count, D)
    cotangent = key_grads.reshape(REPLICAS, row_count, KVW)
    compute = params.astype(jnp.bfloat16)

    def per_replica(packed):
        feats, grads, weight = packed
        produced = (jnp.dot(feats, weight, preferred_element_type=jnp.float32) * factor).astype(jnp.bfloat16)
        gradient = lax.dot_general(feats, grads, (((0,), (0,)), ((), ())), preferred_element_type=jnp.float32) * factor
        return (produced, gradient)
    produced, gradient = lax.map(per_replica, (inputs, cotangent, compute))
    updated = adam_step(params, first_moment, second_moment, gradient, step_index)
    levels = N_REP.bit_length() - 1
    which = (step_index[0] % levels).astype(jnp.int32)
    partner = jnp.bitwise_xor(jnp.arange(REPLICAS, dtype=jnp.int32), jnp.left_shift(jnp.int32(1), which))
    other = jnp.take(updated, partner, axis=0)
    averaged = (0.5 * (updated + other)).astype(jnp.bfloat16)
    return (produced.reshape(TOKENS, KVW), averaged)
```

```python
import functools
import math

import jax
import jax.numpy as jnp
from jax import lax
from jax.experimental import pallas as pl
from jax.experimental.pallas import tpu as pltpu
from jax.sharding import PartitionSpec as P

MESH = pl.DeviceIdType.MESH
beta_one = 0.9
beta_two = 0.95
learn_rate = 0.25
epsilon = 1e-08
PIECES = 4


def step_kernel(
    level, chips, factor, pieces,
    x, g, p, m, v, t,
    key_out, averaged,
    xl, xc, gc, par, mom, var, wall, acc, new, mine, theirs, ksum, kout, aout,
    lsem, xsend, xrecv, gsend, grecv, usend, urecv, dsend, drecv, bsend, brecv, psend, precv, osem,
):
    rep, me = lax.axis_index("rep"), lax.axis_index("fsdp")
    z = me // 2
    core = me - 2 * z
    last = chips - 1
    sib = me + 1 - 2 * core
    mask = 2**level
    mate = rep + mask * (1 - 2 * ((rep // mask) % 2))
    tokens, rows = g.shape[0], p.shape[1]
    piece = rows // pieces
    not_top, not_bottom = z < last, z > 0

    def block(index):
        return pl.ds(pl.multiple_of(index * rows, rows), rows)

    def part(s):
        return pl.ds(pl.multiple_of(s * piece, piece), piece)

    load_p = pltpu.make_async_copy(p.at[0], par, lsem.at[0])
    load_p.start()
    load_x = pltpu.make_async_copy(x, xl, lsem.at[1])
    load_x.start()
    load_g = pltpu.make_async_copy(g, gc.at[pl.ds(0, tokens)], lsem.at[2])
    load_g.start()
    for d in range(chips):
        pltpu.make_async_copy(
            x.at[:, block(2 * d + core)], xc.at[d, pl.ds(0, tokens)], lsem.at[3]
        ).start()
    load_m = pltpu.make_async_copy(m.at[0], mom, lsem.at[4])
    load_m.start()
    load_v = pltpu.make_async_copy(v.at[0], var, lsem.at[5])
    load_v.start()

    barrier = pltpu.get_barrier_semaphore()

    @pl.when(not_top)
    def _():
        pl.semaphore_signal(barrier, inc=1, device_id=(rep, me + 2), device_id_type=MESH)

    @pl.when(not_bottom)
    def _():
        pl.semaphore_signal(barrier, inc=1, device_id=(rep, me - 2), device_id_type=MESH)

    pl.semaphore_signal(barrier, inc=1, device_id=(rep, sib), device_id_type=MESH)
    pl.semaphore_signal(barrier, inc=1, device_id=(mate, me), device_id_type=MESH)
    load_p.wait()
    wall[me] = par[...].astype(jnp.bfloat16)
    pl.semaphore_wait(barrier, 2 + not_top.astype(jnp.int32) + not_bottom.astype(jnp.int32))

    def up(ref, k, s):
        return pltpu.make_async_remote_copy(
            src_ref=ref, dst_ref=ref, send_sem=usend.at[k * pieces + s], recv_sem=urecv.at[k * pieces + s],
            device_id=(rep, me + 2), device_id_type=MESH,
        )

    def down(ref, k, s):
        return pltpu.make_async_remote_copy(
            src_ref=ref, dst_ref=ref, send_sem=dsend.at[k * pieces + s], recv_sem=drecv.at[k * pieces + s],
            device_id=(rep, me - 2), device_id_type=MESH,
        )

    def beside(chip):
        ref = wall.at[2 * chip + core]
        return pltpu.make_async_remote_copy(
            src_ref=ref, dst_ref=ref, send_sem=bsend.at[chip], recv_sem=brecv.at[chip],
            device_id=(rep, sib), device_id_type=MESH,
        )

    def from_beside(chip):
        ref = wall.at[2 * chip + 1 - core]
        return pltpu.make_async_remote_copy(
            src_ref=ref, dst_ref=ref, send_sem=bsend.at[chip], recv_sem=brecv.at[chip],
            device_id=(rep, sib), device_id_type=MESH,
        )

    def to_mate(s):
        return pltpu.make_async_remote_copy(
            src_ref=mine.at[part(s)], dst_ref=theirs.at[part(s)], send_sem=psend.at[s], recv_sem=precv.at[s],
            device_id=(mate, me), device_id_type=MESH,
        )

    for s in range(pieces):

        @pl.when(not_top)
        def _(s=s):
            up(wall.at[me, part(s)], 0, s).start()

        @pl.when(not_bottom)
        def _(s=s):
            down(wall.at[me, part(s)], 0, s).start()

    swap_g = pltpu.make_async_remote_copy(
        src_ref=g, dst_ref=gc.at[pl.ds(tokens, tokens)], send_sem=gsend, recv_sem=grecv,
        device_id=(rep, sib), device_id_type=MESH,
    )
    swap_g.start()
    for d in range(chips):
        pltpu.make_async_remote_copy(
            src_ref=x.at[:, block(2 * d + 1 - core)], dst_ref=xc.at[d, pl.ds(tokens, tokens)],
            send_sem=xsend, recv_sem=xrecv, device_id=(rep, sib), device_id_type=MESH,
        ).start()
    beside(z).start()
    load_x.wait()
    load_g.wait()
    load_m.wait()
    load_v.wait()
    whole = pltpu.make_async_remote_copy(
        src_ref=xc.at[:, pl.ds(0, tokens)], dst_ref=xc.at[:, pl.ds(tokens, tokens)],
        send_sem=xsend, recv_sem=xrecv, device_id=(rep, sib), device_id_type=MESH,
    )
    pltpu.make_async_copy(
        xc.at[:, pl.ds(0, tokens)], xc.at[:, pl.ds(0, tokens)], lsem.at[3]
    ).wait()
    whole.wait()
    swap_g.wait()

    def project(index):
        ksum[...] += jnp.dot(xl[:, block(index)], wall[index], preferred_element_type=jnp.float32)

    ksum[...] = jnp.dot(xl[:, block(me)], wall[me], preferred_element_type=jnp.float32)

    def partial(d, s):
        return lax.dot_general(
            xc[d, :, part(s)], gc[...], (((0,), (0,)), ((), ())), preferred_element_type=jnp.float32
        )

    def add_to(slot, d, s, received):
        own = partial(d, s)

        @pl.when(received)
        def _():
            acc[slot, part(s), :] = (own + acc[slot, part(s), :].astype(jnp.float32)).astype(jnp.bfloat16)

        @pl.when(jnp.logical_not(received))
        def _():
            acc[slot, part(s), :] = own.astype(jnp.bfloat16)

    def turn(i, carry):
        k, s = i // pieces, i % pieces

        @pl.when(k <= z)
        def _():
            chip = z - k
            ref = wall.at[2 * chip + core, part(s)]
            up(ref, k - 1, s).wait_recv()

            @pl.when(not_top)
            def _():
                up(ref, k, s).start()

        @pl.when(k <= last - z)
        def _():
            chip = z + k
            ref = wall.at[2 * chip + core, part(s)]
            down(ref, k - 1, s).wait_recv()

            @pl.when(not_bottom)
            def _():
                down(ref, k, s).start()

        @pl.when(k > z)
        def _():
            d = chips + z - k
            ref = acc.at[d + 1, part(s)]

            @pl.when(not_bottom)
            def _():
                up(ref, k - 1, s).wait_recv()

            add_to(d + 1, d, s, not_bottom)
            up(ref, k, s).start()

        @pl.when(k > last - z)
        def _():
            d = z + k - chips
            ref = acc.at[d, part(s)]

            @pl.when(not_top)
            def _():
                down(ref, k - 1, s).wait_recv()

            add_to(d, d, s, not_top)
            down(ref, k, s).start()

        @pl.when(s == pieces - 1)
        def _():
            @pl.when(k <= z)
            def _():
                beside(z - k).start()
                project(2 * (z - k) + core)

            @pl.when(k <= last - z)
            def _():
                beside(z + k).start()
                project(2 * (z + k) + core)

            @pl.when(k - 1 <= z)
            def _():
                from_beside(z - k + 1).wait_recv()
                project(2 * (z - k + 1) + 1 - core)

            @pl.when(jnp.logical_and(k > 1, k - 1 <= last - z))
            def _():
                from_beside(z + k - 1).wait_recv()
                project(2 * (z + k - 1) + 1 - core)

        return carry

    lax.fori_loop(pieces, chips * pieces, turn, 0)

    @pl.when(z == last)
    def _():
        from_beside(0).wait_recv()
        project(1 - core)

    @pl.when(z == 0)
    def _():
        from_beside(last).wait_recv()
        project(2 * last + 1 - core)

    kout[...] = (ksum[...] * factor).astype(jnp.bfloat16)
    store_k = pltpu.make_async_copy(kout, key_out, osem.at[pieces])
    store_k.start()

    steps = jnp.full((1, g.shape[1]), t[0] + 1, jnp.int32).astype(jnp.float32)
    corr_one = 1.0 - jnp.exp(steps * math.log(beta_one))
    corr_two = 1.0 - jnp.exp(steps * math.log(beta_two))

    def finish(s, carry):
        new[part(s), :] = partial(z, s)

        @pl.when(not_bottom)
        def _():
            up(acc.at[z + 1, part(s)], last, s).wait_recv()
            new[part(s), :] += acc[z + 1, part(s), :].astype(jnp.float32)

        @pl.when(not_top)
        def _():
            down(acc.at[z, part(s)], last, s).wait_recv()
            new[part(s), :] += acc[z, part(s), :].astype(jnp.float32)

        gradient = new[part(s), :] * factor
        one = beta_one * mom[part(s), :].astype(jnp.float32) + (1.0 - beta_one) * gradient
        two = beta_two * var[part(s), :].astype(jnp.float32) + (1.0 - beta_two) * gradient * gradient
        updated = par[part(s), :] - learn_rate * (one / corr_one) / (jnp.sqrt(two / corr_two) + epsilon)
        new[part(s), :] = updated
        mine[part(s), :] = updated.astype(jnp.bfloat16)
        to_mate(s).start()
        return carry

    lax.fori_loop(0, pieces, finish, 0)

    def store_a(s):
        return pltpu.make_async_copy(aout.at[part(s)], averaged.at[0, part(s)], osem.at[s])

    def average(s, carry):
        to_mate(s).wait_recv()
        aout[part(s), :] = (0.5 * (new[part(s), :] + theirs[part(s), :].astype(jnp.float32))).astype(jnp.bfloat16)
        store_a(s).start()
        return carry

    lax.fori_loop(0, pieces, average, 0)

    def sent(i, carry):
        k, s = i // pieces, i % pieces

        @pl.when(not_top)
        def _():
            up(acc.at[0, part(s)], k, s).wait_send()

        @pl.when(not_bottom)
        def _():
            down(acc.at[0, part(s)], k, s).wait_send()

        return carry

    lax.fori_loop(0, chips * pieces, sent, 0)
    for chip in range(chips):
        beside(chip).wait_send()
    for s in range(pieces):
        to_mate(s).wait_send()
        store_a(s).wait()
    store_k.wait()


def call(level, chips, factor, x, g, p, m, v, t):
    tokens, width = g.shape
    rows = p.shape[1]
    pieces = PIECES
    dma = pltpu.SemaphoreType.DMA
    any_space = pl.BlockSpec(memory_space=pl.ANY)
    return pl.pallas_call(
        functools.partial(step_kernel, level, chips, factor, pieces),
        out_shape=(
            jax.ShapeDtypeStruct((tokens, width), jnp.bfloat16),
            jax.ShapeDtypeStruct((1, rows, width), jnp.bfloat16),
        ),
        in_specs=[any_space] * 5 + [pl.BlockSpec(memory_space=pltpu.SMEM)],
        out_specs=(any_space, any_space),
        scratch_shapes=[
            pltpu.VMEM(x.shape, jnp.bfloat16),
            pltpu.VMEM((chips, 2 * tokens, rows), jnp.bfloat16),
            pltpu.VMEM((2 * tokens, width), jnp.bfloat16),
            pltpu.VMEM((rows, width), jnp.float32),
            pltpu.VMEM((rows, width), jnp.bfloat16),
            pltpu.VMEM((rows, width), jnp.bfloat16),
            pltpu.VMEM((2 * chips, rows, width), jnp.bfloat16),
            pltpu.VMEM((chips + 1, rows, width), jnp.bfloat16),
            pltpu.VMEM((rows, width), jnp.float32),
            pltpu.VMEM((rows, width), jnp.bfloat16),
            pltpu.VMEM((rows, width), jnp.bfloat16),
            pltpu.VMEM((tokens, width), jnp.float32),
            pltpu.VMEM((tokens, width), jnp.bfloat16),
            pltpu.VMEM((rows, width), jnp.bfloat16),
            dma((6,)),
            dma, dma, dma, dma,
            dma((chips * pieces,)), dma((chips * pieces,)),
            dma((chips * pieces,)), dma((chips * pieces,)),
            dma((chips,)), dma((chips,)),
            dma((pieces,)), dma((pieces,)),
            dma((pieces + 1,)),
        ],
        compiler_params=pltpu.CompilerParams(
            collective_id=level, has_side_effects=True, vmem_limit_bytes=48 * 2**20
        ),
        cost_estimate=pl.CostEstimate(
            flops=4 * tokens * width * x.shape[1], bytes_accessed=6 * 2**20, transcendentals=0
        ),
        name=f"level_{level}",
    )(x, g, p, m, v, t)


def per_device(activations, key_grads, params, first_moment, second_moment, step_index):
    factor = activations.shape[1] ** (-0.5)
    chips = lax.axis_size("fsdp") // 2
    levels = lax.axis_size("rep").bit_length() - 1
    branches = [functools.partial(call, level, chips, factor) for level in range(levels)]
    return lax.switch(
        step_index[0] % levels, branches, activations, key_grads, params, first_moment, second_moment, step_index
    )


def solution(mesh):
    in_specs = (
        P(("rep", "fsdp"), None),
        P(("rep", "fsdp"), None),
        P("rep", "fsdp", None),
        P("rep", "fsdp", None),
        P("rep", "fsdp", None),
        P(),
    )
    out_specs = (P(("rep", "fsdp"), None), P("rep", "fsdp", None))
    return jax.shard_map(
        per_device, mesh=mesh, in_specs=in_specs, out_specs=out_specs, check_vma=False
    )
```

```python
import functools
import math

import jax
import jax.numpy as jnp
from jax import lax
from jax.experimental import pallas as pl
from jax.experimental.pallas import tpu as pltpu
from jax.sharding import PartitionSpec as P

MESH = pl.DeviceIdType.MESH
beta_one = 0.9
beta_two = 0.95
learn_rate = 0.25
epsilon = 1e-08
PIECES = 2
TAIL = 8


def step_kernel(
    level, chips, factor, pieces, tail,
    x, g, p, m, v, t,
    key_out, averaged,
    xl, xc, gc, par, mom, var, wall, acc, new, mine, theirs, ksum, kout, aout,
    fsem, lsem, xsend, xrecv, gsend, grecv, usend, urecv, dsend, drecv, bsend, brecv, psend, precv, osem,
):
    rep, me = lax.axis_index("rep"), lax.axis_index("fsdp")
    z = me // 2
    core = me - 2 * z
    last = chips - 1
    sib = me + 1 - 2 * core
    mask = 2**level
    mate = rep + mask * (1 - 2 * ((rep // mask) % 2))
    tokens, rows = g.shape[0], p.shape[1]
    piece, small = rows // pieces, rows // tail
    split = tail // pieces
    not_top, not_bottom = z < last, z > 0

    def block(index):
        return pl.ds(pl.multiple_of(index * rows, rows), rows)

    def part(s):
        return pl.ds(pl.multiple_of(s * piece, piece), piece)

    def bit(j):
        return pl.ds(pl.multiple_of(j * small, small), small)

    barrier = pltpu.get_barrier_semaphore()

    @pl.when(not_top)
    def _():
        pl.semaphore_signal(barrier, inc=1, device_id=(rep, me + 2), device_id_type=MESH)

    @pl.when(not_bottom)
    def _():
        pl.semaphore_signal(barrier, inc=1, device_id=(rep, me - 2), device_id_type=MESH)

    pl.semaphore_signal(barrier, inc=1, device_id=(rep, sib), device_id_type=MESH)
    pl.semaphore_signal(barrier, inc=1, device_id=(mate, me), device_id_type=MESH)

    load_p = [pltpu.make_async_copy(p.at[0, part(s)], par.at[part(s)], fsem.at[s]) for s in range(pieces)]
    for s in range(pieces):
        load_p[s].start()
    load_x = pltpu.make_async_copy(x, xl, lsem.at[1])
    load_x.start()
    load_g = pltpu.make_async_copy(g, gc.at[pl.ds(0, tokens)], lsem.at[2])
    load_g.start()
    for d in range(chips):
        pltpu.make_async_copy(
            x.at[:, block(2 * d + core)], xc.at[d, pl.ds(0, tokens)], lsem.at[3]
        ).start()
    load_m = pltpu.make_async_copy(m.at[0], mom, lsem.at[4])
    load_m.start()
    load_v = pltpu.make_async_copy(v.at[0], var, lsem.at[5])
    load_v.start()

    def up(ref, k, s):
        return pltpu.make_async_remote_copy(
            src_ref=ref, dst_ref=ref, send_sem=usend.at[k * pieces + s], recv_sem=urecv.at[k * pieces + s],
            device_id=(rep, me + 2), device_id_type=MESH,
        )

    def down(ref, k, s):
        return pltpu.make_async_remote_copy(
            src_ref=ref, dst_ref=ref, send_sem=dsend.at[k * pieces + s], recv_sem=drecv.at[k * pieces + s],
            device_id=(rep, me - 2), device_id_type=MESH,
        )

    def up_last(j):
        ref = acc.at[z + 2, bit(j)]
        return pltpu.make_async_remote_copy(
            src_ref=ref, dst_ref=ref, send_sem=usend.at[last * pieces + j], recv_sem=urecv.at[last * pieces + j],
            device_id=(rep, me + 2), device_id_type=MESH,
        )

    def down_last(j):
        ref = acc.at[z - 1, bit(j)]
        return pltpu.make_async_remote_copy(
            src_ref=ref, dst_ref=ref, send_sem=dsend.at[last * pieces + j], recv_sem=drecv.at[last * pieces + j],
            device_id=(rep, me - 2), device_id_type=MESH,
        )

    def up_from(j):
        ref = acc.at[z + 1, bit(j)]
        return pltpu.make_async_remote_copy(
            src_ref=ref, dst_ref=ref, send_sem=usend.at[last * pieces + j], recv_sem=urecv.at[last * pieces + j],
            device_id=(rep, me - 2), device_id_type=MESH,
        )

    def down_from(j):
        ref = acc.at[z, bit(j)]
        return pltpu.make_async_remote_copy(
            src_ref=ref, dst_ref=ref, send_sem=dsend.at[last * pieces + j], recv_sem=drecv.at[last * pieces + j],
            device_id=(rep, me + 2), device_id_type=MESH,
        )

    def beside(chip):
        ref = wall.at[2 * chip + core]
        return pltpu.make_async_remote_copy(
            src_ref=ref, dst_ref=ref, send_sem=bsend.at[chip], recv_sem=brecv.at[chip],
            device_id=(rep, sib), device_id_type=MESH,
        )

    def from_beside(chip):
        ref = wall.at[2 * chip + 1 - core]
        return pltpu.make_async_remote_copy(
            src_ref=ref, dst_ref=ref, send_sem=bsend.at[chip], recv_sem=brecv.at[chip],
            device_id=(rep, sib), device_id_type=MESH,
        )

    def to_mate(s):
        return pltpu.make_async_remote_copy(
            src_ref=mine.at[bit(s)], dst_ref=theirs.at[bit(s)], send_sem=psend.at[s], recv_sem=precv.at[s],
            device_id=(mate, me), device_id_type=MESH,
        )

    for s in range(pieces):
        load_p[s].wait()
        wall[me, part(s)] = par[part(s), :].astype(jnp.bfloat16)
        if s == 0:
            pl.semaphore_wait(barrier, 2 + not_top.astype(jnp.int32) + not_bottom.astype(jnp.int32))

        @pl.when(not_top)
        def _(s=s):
            up(wall.at[me, part(s)], 0, s).start()

        @pl.when(not_bottom)
        def _(s=s):
            down(wall.at[me, part(s)], 0, s).start()

    swap_g = pltpu.make_async_remote_copy(
        src_ref=g, dst_ref=gc.at[pl.ds(tokens, tokens)], send_sem=gsend, recv_sem=grecv,
        device_id=(rep, sib), device_id_type=MESH,
    )
    swap_g.start()
    for d in range(chips):
        pltpu.make_async_remote_copy(
            src_ref=x.at[:, block(2 * d + 1 - core)], dst_ref=xc.at[d, pl.ds(tokens, tokens)],
            send_sem=xsend, recv_sem=xrecv, device_id=(rep, sib), device_id_type=MESH,
        ).start()
    beside(z).start()
    load_x.wait()
    load_g.wait()
    load_m.wait()
    load_v.wait()
    whole = pltpu.make_async_remote_copy(
        src_ref=xc.at[:, pl.ds(0, tokens)], dst_ref=xc.at[:, pl.ds(tokens, tokens)],
        send_sem=xsend, recv_sem=xrecv, device_id=(rep, sib), device_id_type=MESH,
    )
    pltpu.make_async_copy(
        xc.at[:, pl.ds(0, tokens)], xc.at[:, pl.ds(0, tokens)], lsem.at[3]
    ).wait()
    whole.wait()
    swap_g.wait()

    def project(index):
        ksum[...] += jnp.dot(xl[:, block(index)], wall[index], preferred_element_type=jnp.float32)

    ksum[...] = jnp.dot(xl[:, block(me)], wall[me], preferred_element_type=jnp.float32)

    def partial(d, s):
        return lax.dot_general(
            xc[d, :, part(s)], gc[...], (((0,), (0,)), ((), ())), preferred_element_type=jnp.float32
        )

    def add_to(slot, d, s, received):
        own = partial(d, s)

        @pl.when(received)
        def _():
            acc[slot, part(s), :] = (own + acc[slot, part(s), :].astype(jnp.float32)).astype(jnp.bfloat16)

        @pl.when(jnp.logical_not(received))
        def _():
            acc[slot, part(s), :] = own.astype(jnp.bfloat16)

    def turn(i, carry):
        k, s = i // pieces, i % pieces

        @pl.when(k <= z)
        def _():
            chip = z - k
            ref = wall.at[2 * chip + core, part(s)]
            up(ref, k - 1, s).wait_recv()

            @pl.when(not_top)
            def _():
                up(ref, k, s).start()

        @pl.when(k <= last - z)
        def _():
            chip = z + k
            ref = wall.at[2 * chip + core, part(s)]
            down(ref, k - 1, s).wait_recv()

            @pl.when(not_bottom)
            def _():
                down(ref, k, s).start()

        @pl.when(k > z)
        def _():
            d = chips + z - k
            ref = acc.at[d + 1, part(s)]

            @pl.when(not_bottom)
            def _():
                up(ref, k - 1, s).wait_recv()

            add_to(d + 1, d, s, not_bottom)

            @pl.when(k < last)
            def _():
                up(ref, k, s).start()

            @pl.when(k == last)
            def _():
                for q in range(split):
                    up_last(s * split + q).start()

        @pl.when(k > last - z)
        def _():
            d = z + k - chips
            ref = acc.at[d, part(s)]

            @pl.when(not_top)
            def _():
                down(ref, k - 1, s).wait_recv()

            add_to(d, d, s, not_top)

            @pl.when(k < last)
            def _():
                down(ref, k, s).start()

            @pl.when(k == last)
            def _():
                for q in range(split):
                    down_last(s * split + q).start()

        @pl.when(s == pieces - 1)
        def _():
            @pl.when(k <= z)
            def _():
                beside(z - k).start()
                project(2 * (z - k) + core)

            @pl.when(k <= last - z)
            def _():
                beside(z + k).start()
                project(2 * (z + k) + core)

            @pl.when(k - 1 <= z)
            def _():
                from_beside(z - k + 1).wait_recv()
                project(2 * (z - k + 1) + 1 - core)

            @pl.when(jnp.logical_and(k > 1, k - 1 <= last - z))
            def _():
                from_beside(z + k - 1).wait_recv()
                project(2 * (z + k - 1) + 1 - core)

        return carry

    lax.fori_loop(pieces, chips * pieces, turn, 0)

    def own_term(s, carry):
        new[part(s), :] = partial(z, s)
        return carry

    lax.fori_loop(0, pieces, own_term, 0)

    @pl.when(z == last)
    def _():
        from_beside(0).wait_recv()
        project(1 - core)

    @pl.when(z == 0)
    def _():
        from_beside(last).wait_recv()
        project(2 * last + 1 - core)

    kout[...] = (ksum[...] * factor).astype(jnp.bfloat16)
    store_k = pltpu.make_async_copy(kout, key_out, osem.at[tail])
    store_k.start()

    steps = jnp.full((1, g.shape[1]), t[0] + 1, jnp.int32).astype(jnp.float32)
    corr_one = 1.0 - jnp.exp(steps * math.log(beta_one))
    corr_two = 1.0 - jnp.exp(steps * math.log(beta_two))

    def finish(j, carry):
        at = bit(j)
        own = new[at, :]

        @pl.when(not_bottom)
        def _():
            up_from(j).wait_recv()

        @pl.when(not_top)
        def _():
            down_from(j).wait_recv()

        below = jnp.where(not_bottom, acc[z + 1, at, :].astype(jnp.float32), 0.0)
        above = jnp.where(not_top, acc[z, at, :].astype(jnp.float32), 0.0)
        gradient = (own + below + above) * factor
        one = beta_one * mom[at, :].astype(jnp.float32) + (1.0 - beta_one) * gradient
        two = beta_two * var[at, :].astype(jnp.float32) + (1.0 - beta_two) * gradient * gradient
        updated = par[at, :] - learn_rate * (one / corr_one) / (jnp.sqrt(two / corr_two) + epsilon)
        new[at, :] = updated
        mine[at, :] = updated.astype(jnp.bfloat16)
        to_mate(j).start()
        return carry

    lax.fori_loop(0, tail, finish, 0)

    def store_a(j):
        return pltpu.make_async_copy(aout.at[bit(j)], averaged.at[0, bit(j)], osem.at[j])

    def average(j, carry):
        to_mate(j).wait_recv()
        aout[bit(j), :] = (0.5 * (new[bit(j), :] + theirs[bit(j), :].astype(jnp.float32))).astype(jnp.bfloat16)
        store_a(j).start()
        return carry

    lax.fori_loop(0, tail, average, 0)

    def sent(i, carry):
        k, s = i // pieces, i % pieces

        @pl.when(not_top)
        def _():
            up(acc.at[0, part(s)], k, s).wait_send()

        @pl.when(not_bottom)
        def _():
            down(acc.at[0, part(s)], k, s).wait_send()

        return carry

    def sent_last(j, carry):
        @pl.when(not_top)
        def _():
            up_last(j).wait_send()

        @pl.when(not_bottom)
        def _():
            down_last(j).wait_send()

        to_mate(j).wait_send()
        store_a(j).wait()
        return carry

    lax.fori_loop(0, last * pieces, sent, 0)
    for chip in range(chips):
        beside(chip).wait_send()
    lax.fori_loop(0, tail, sent_last, 0)
    store_k.wait()


def call(level, chips, factor, x, g, p, m, v, t):
    tokens, width = g.shape
    rows = p.shape[1]
    pieces, tail = PIECES, TAIL
    dma = pltpu.SemaphoreType.DMA
    any_space = pl.BlockSpec(memory_space=pl.ANY)
    return pl.pallas_call(
        functools.partial(step_kernel, level, chips, factor, pieces, tail),
        out_shape=(
            jax.ShapeDtypeStruct((tokens, width), jnp.bfloat16),
            jax.ShapeDtypeStruct((1, rows, width), jnp.bfloat16),
        ),
        in_specs=[any_space] * 5 + [pl.BlockSpec(memory_space=pltpu.SMEM)],
        out_specs=(any_space, any_space),
        scratch_shapes=[
            pltpu.VMEM(x.shape, jnp.bfloat16),
            pltpu.VMEM((chips, 2 * tokens, rows), jnp.bfloat16),
            pltpu.VMEM((2 * tokens, width), jnp.bfloat16),
            pltpu.VMEM((rows, width), jnp.float32),
            pltpu.VMEM((rows, width), jnp.bfloat16),
            pltpu.VMEM((rows, width), jnp.bfloat16),
            pltpu.VMEM((2 * chips, rows, width), jnp.bfloat16),
            pltpu.VMEM((chips + 1, rows, width), jnp.bfloat16),
            pltpu.VMEM((rows, width), jnp.float32),
            pltpu.VMEM((rows, width), jnp.bfloat16),
            pltpu.VMEM((rows, width), jnp.bfloat16),
            pltpu.VMEM((tokens, width), jnp.float32),
            pltpu.VMEM((tokens, width), jnp.bfloat16),
            pltpu.VMEM((rows, width), jnp.bfloat16),
            dma((pieces,)), dma((6,)),
            dma, dma, dma, dma,
            dma(((chips - 1) * pieces + tail,)), dma(((chips - 1) * pieces + tail,)),
            dma(((chips - 1) * pieces + tail,)), dma(((chips - 1) * pieces + tail,)),
            dma((chips,)), dma((chips,)),
            dma((tail,)), dma((tail,)),
            dma((tail + 1,)),
        ],
        compiler_params=pltpu.CompilerParams(
            collective_id=level, has_side_effects=True, vmem_limit_bytes=48 * 2**20
        ),
        cost_estimate=pl.CostEstimate(
            flops=4 * tokens * width * x.shape[1], bytes_accessed=6 * 2**20, transcendentals=0
        ),
        name=f"level_{level}",
    )(x, g, p, m, v, t)


def emit_kernel(first, second, first_out, second_out, sem):
    copies = [
        pltpu.make_async_copy(first, first_out, sem.at[0]),
        pltpu.make_async_copy(second, second_out, sem.at[1]),
    ]
    for copy in copies:
        copy.start()
    for copy in copies:
        copy.wait()


def emit(first, second):
    any_space = pl.BlockSpec(memory_space=pl.ANY)
    return pl.pallas_call(
        emit_kernel,
        out_shape=(
            jax.ShapeDtypeStruct(first.shape, first.dtype),
            jax.ShapeDtypeStruct(second.shape, second.dtype),
        ),
        in_specs=[any_space] * 2,
        out_specs=(any_space, any_space),
        scratch_shapes=[pltpu.SemaphoreType.DMA((2,))],
        name="emit",
    )(first, second)


def per_device(activations, key_grads, params, first_moment, second_moment, step_index):
    factor = activations.shape[1] ** (-0.5)
    chips = lax.axis_size("fsdp") // 2
    levels = lax.axis_size("rep").bit_length() - 1
    branches = [functools.partial(call, level, chips, factor) for level in range(levels)]
    key_out, averaged = lax.switch(
        lax.rem(step_index[0], levels), branches,
        activations, key_grads, params, first_moment, second_moment, step_index,
    )
    return emit(key_out, averaged)


def solution(mesh):
    in_specs = (
        P(("rep", "fsdp"), None),
        P(("rep", "fsdp"), None),
        P("rep", "fsdp", None),
        P("rep", "fsdp", None),
        P("rep", "fsdp", None),
        P(),
    )
    out_specs = (P(("rep", "fsdp"), None), P("rep", "fsdp", None))
    return jax.shard_map(
        per_device, mesh=mesh, in_specs=in_specs, out_specs=out_specs, check_vma=False
    )
```

```python
import functools
import math

import jax
import jax.numpy as jnp
from jax import lax
from jax.experimental import pallas as pl
from jax.experimental.pallas import tpu as pltpu
from jax.sharding import PartitionSpec as P

MESH = pl.DeviceIdType.MESH
beta_one = 0.9
beta_two = 0.95
learn_rate = 0.25
epsilon = 1e-08
PIECES = 2
TAIL = 4


def step_kernel(
    level, chips, factor, pieces, tail,
    x, g, p, m, v, t,
    key_out, averaged,
    xl, xc, gc, par, mom, var, wall, acc, new, mine, theirs, ksum,
    fsem, lsem, xsend, xrecv, gsend, grecv, usend, urecv, dsend, drecv, bsend, brecv, psend, precv,
):
    rep, me = lax.axis_index("rep"), lax.axis_index("fsdp")
    z = me // 2
    core = me - 2 * z
    last = chips - 1
    sib = me + 1 - 2 * core
    mask = 2**level
    mate = rep + mask * (1 - 2 * ((rep // mask) % 2))
    tokens, rows = g.shape[0], p.shape[1]
    piece, small = rows // pieces, rows // tail
    split = tail // pieces
    not_top, not_bottom = z < last, z > 0

    def block(index):
        return pl.ds(pl.multiple_of(index * rows, rows), rows)

    def part(s):
        return pl.ds(pl.multiple_of(s * piece, piece), piece)

    def bit(j):
        return pl.ds(pl.multiple_of(j * small, small), small)

    load_p = [pltpu.make_async_copy(p.at[0, part(s)], par.at[part(s)], fsem.at[s]) for s in range(pieces)]
    load_p[0].start()
    barrier = pltpu.get_barrier_semaphore()

    @pl.when(not_top)
    def _():
        pl.semaphore_signal(barrier, inc=1, device_id=(rep, me + 2), device_id_type=MESH)

    @pl.when(not_bottom)
    def _():
        pl.semaphore_signal(barrier, inc=1, device_id=(rep, me - 2), device_id_type=MESH)

    pl.semaphore_signal(barrier, inc=1, device_id=(rep, sib), device_id_type=MESH)
    pl.semaphore_signal(barrier, inc=1, device_id=(mate, me), device_id_type=MESH)

    for s in range(1, pieces):
        load_p[s].start()
    load_x = pltpu.make_async_copy(x, xl, lsem.at[1])
    load_x.start()
    load_g = pltpu.make_async_copy(g, gc.at[pl.ds(0, tokens)], lsem.at[2])
    load_g.start()
    for d in range(chips):
        pltpu.make_async_copy(
            x.at[:, block(2 * d + core)], xc.at[d, pl.ds(0, tokens)], lsem.at[3]
        ).start()
    load_m = pltpu.make_async_copy(m.at[0], mom, lsem.at[4])
    load_m.start()
    load_v = pltpu.make_async_copy(v.at[0], var, lsem.at[5])
    load_v.start()

    def up(ref, k, s):
        return pltpu.make_async_remote_copy(
            src_ref=ref, dst_ref=ref, send_sem=usend.at[k * pieces + s], recv_sem=urecv.at[k * pieces + s],
            device_id=(rep, me + 2), device_id_type=MESH,
        )

    def down(ref, k, s):
        return pltpu.make_async_remote_copy(
            src_ref=ref, dst_ref=ref, send_sem=dsend.at[k * pieces + s], recv_sem=drecv.at[k * pieces + s],
            device_id=(rep, me - 2), device_id_type=MESH,
        )

    def up_last(j):
        ref = acc.at[z + 2, bit(j)]
        return pltpu.make_async_remote_copy(
            src_ref=ref, dst_ref=ref, send_sem=usend.at[last * pieces + j], recv_sem=urecv.at[last * pieces + j],
            device_id=(rep, me + 2), device_id_type=MESH,
        )

    def down_last(j):
        ref = acc.at[z - 1, bit(j)]
        return pltpu.make_async_remote_copy(
            src_ref=ref, dst_ref=ref, send_sem=dsend.at[last * pieces + j], recv_sem=drecv.at[last * pieces + j],
            device_id=(rep, me - 2), device_id_type=MESH,
        )

    def up_from(j):
        ref = acc.at[z + 1, bit(j)]
        return pltpu.make_async_remote_copy(
            src_ref=ref, dst_ref=ref, send_sem=usend.at[last * pieces + j], recv_sem=urecv.at[last * pieces + j],
            device_id=(rep, me - 2), device_id_type=MESH,
        )

    def down_from(j):
        ref = acc.at[z, bit(j)]
        return pltpu.make_async_remote_copy(
            src_ref=ref, dst_ref=ref, send_sem=dsend.at[last * pieces + j], recv_sem=drecv.at[last * pieces + j],
            device_id=(rep, me + 2), device_id_type=MESH,
        )

    def beside(chip):
        ref = wall.at[2 * chip + core]
        return pltpu.make_async_remote_copy(
            src_ref=ref, dst_ref=ref, send_sem=bsend.at[chip], recv_sem=brecv.at[chip],
            device_id=(rep, sib), device_id_type=MESH,
        )

    def from_beside(chip):
        ref = wall.at[2 * chip + 1 - core]
        return pltpu.make_async_remote_copy(
            src_ref=ref, dst_ref=ref, send_sem=bsend.at[chip], recv_sem=brecv.at[chip],
            device_id=(rep, sib), device_id_type=MESH,
        )

    def to_mate(j):
        return pltpu.make_async_remote_copy(
            src_ref=mine.at[bit(j)], dst_ref=theirs.at[bit(j)], send_sem=psend.at[j], recv_sem=precv.at[j],
            device_id=(mate, me), device_id_type=MESH,
        )

    for s in range(pieces):
        load_p[s].wait()
        wall[me, part(s)] = par[part(s), :].astype(jnp.bfloat16)
        if s == 0:
            pl.semaphore_wait(barrier, 2 + not_top.astype(jnp.int32) + not_bottom.astype(jnp.int32))

        @pl.when(not_top)
        def _(s=s):
            up(wall.at[me, part(s)], 0, s).start()

        @pl.when(not_bottom)
        def _(s=s):
            down(wall.at[me, part(s)], 0, s).start()

    swap_g = pltpu.make_async_remote_copy(
        src_ref=g, dst_ref=gc.at[pl.ds(tokens, tokens)], send_sem=gsend, recv_sem=grecv,
        device_id=(rep, sib), device_id_type=MESH,
    )
    swap_g.start()
    for d in range(chips):
        pltpu.make_async_remote_copy(
            src_ref=x.at[:, block(2 * d + 1 - core)], dst_ref=xc.at[d, pl.ds(tokens, tokens)],
            send_sem=xsend, recv_sem=xrecv, device_id=(rep, sib), device_id_type=MESH,
        ).start()
    beside(z).start()
    load_x.wait()
    load_g.wait()
    load_m.wait()
    load_v.wait()
    whole = pltpu.make_async_remote_copy(
        src_ref=xc.at[:, pl.ds(0, tokens)], dst_ref=xc.at[:, pl.ds(tokens, tokens)],
        send_sem=xsend, recv_sem=xrecv, device_id=(rep, sib), device_id_type=MESH,
    )
    pltpu.make_async_copy(
        xc.at[:, pl.ds(0, tokens)], xc.at[:, pl.ds(0, tokens)], lsem.at[3]
    ).wait()
    whole.wait()
    swap_g.wait()

    def project(index):
        ksum[...] += jnp.dot(xl[:, block(index)], wall[index], preferred_element_type=jnp.float32)

    ksum[...] = jnp.dot(xl[:, block(me)], wall[me], preferred_element_type=jnp.float32)

    def partial(d, s):
        return lax.dot_general(
            xc[d, :, part(s)], gc[...], (((0,), (0,)), ((), ())), preferred_element_type=jnp.float32
        )

    def add_to(slot, d, s, received):
        own = partial(d, s)

        @pl.when(received)
        def _():
            acc[slot, part(s), :] = (own + acc[slot, part(s), :].astype(jnp.float32)).astype(jnp.bfloat16)

        @pl.when(jnp.logical_not(received))
        def _():
            acc[slot, part(s), :] = own.astype(jnp.bfloat16)

    def turn(i, carry):
        k, s = i // pieces, i % pieces

        @pl.when(k <= z)
        def _():
            chip = z - k
            ref = wall.at[2 * chip + core, part(s)]
            up(ref, k - 1, s).wait_recv()

            @pl.when(not_top)
            def _():
                up(ref, k, s).start()

        @pl.when(k <= last - z)
        def _():
            chip = z + k
            ref = wall.at[2 * chip + core, part(s)]
            down(ref, k - 1, s).wait_recv()

            @pl.when(not_bottom)
            def _():
                down(ref, k, s).start()

        @pl.when(k > z)
        def _():
            d = chips + z - k
            ref = acc.at[d + 1, part(s)]

            @pl.when(not_bottom)
            def _():
                up(ref, k - 1, s).wait_recv()

            add_to(d + 1, d, s, not_bottom)

            @pl.when(k < last)
            def _():
                up(ref, k, s).start()

            @pl.when(k == last)
            def _():
                for q in range(split):
                    up_last(s * split + q).start()

        @pl.when(k > last - z)
        def _():
            d = z + k - chips
            ref = acc.at[d, part(s)]

            @pl.when(not_top)
            def _():
                down(ref, k - 1, s).wait_recv()

            add_to(d, d, s, not_top)

            @pl.when(k < last)
            def _():
                down(ref, k, s).start()

            @pl.when(k == last)
            def _():
                for q in range(split):
                    down_last(s * split + q).start()

        @pl.when(s == pieces - 1)
        def _():
            @pl.when(k <= z)
            def _():
                beside(z - k).start()
                project(2 * (z - k) + core)

            @pl.when(k <= last - z)
            def _():
                beside(z + k).start()
                project(2 * (z + k) + core)

            @pl.when(k - 1 <= z)
            def _():
                from_beside(z - k + 1).wait_recv()
                project(2 * (z - k + 1) + 1 - core)

            @pl.when(jnp.logical_and(k > 1, k - 1 <= last - z))
            def _():
                from_beside(z + k - 1).wait_recv()
                project(2 * (z + k - 1) + 1 - core)

        return carry

    lax.fori_loop(pieces, chips * pieces, turn, 0)

    def own_term(s, carry):
        new[part(s), :] = partial(z, s)
        return carry

    lax.fori_loop(0, pieces, own_term, 0)

    @pl.when(z == last)
    def _():
        from_beside(0).wait_recv()
        project(1 - core)

    @pl.when(z == 0)
    def _():
        from_beside(last).wait_recv()
        project(2 * last + 1 - core)

    key_out[...] = (ksum[...] * factor).astype(jnp.bfloat16)

    steps = jnp.full((1, g.shape[1]), t[0] + 1, jnp.int32).astype(jnp.float32)
    corr_one = 1.0 - jnp.exp(steps * math.log(beta_one))
    corr_two = 1.0 - jnp.exp(steps * math.log(beta_two))

    def finish(j, carry):
        at = bit(j)
        own = new[at, :]

        @pl.when(not_bottom)
        def _():
            up_from(j).wait_recv()

        @pl.when(not_top)
        def _():
            down_from(j).wait_recv()

        below = jnp.where(not_bottom, acc[z + 1, at, :].astype(jnp.float32), 0.0)
        above = jnp.where(not_top, acc[z, at, :].astype(jnp.float32), 0.0)
        gradient = (own + below + above) * factor
        one = beta_one * mom[at, :].astype(jnp.float32) + (1.0 - beta_one) * gradient
        two = beta_two * var[at, :].astype(jnp.float32) + (1.0 - beta_two) * gradient * gradient
        updated = par[at, :] - learn_rate * (one / corr_one) / (jnp.sqrt(two / corr_two) + epsilon)
        new[at, :] = updated
        mine[at, :] = updated.astype(jnp.bfloat16)
        to_mate(j).start()
        return carry

    lax.fori_loop(0, tail, finish, 0)

    def sent(i, carry):
        k, s = i // pieces, i % pieces

        @pl.when(not_top)
        def _():
            up(acc.at[0, part(s)], k, s).wait_send()

        @pl.when(not_bottom)
        def _():
            down(acc.at[0, part(s)], k, s).wait_send()

        return carry

    lax.fori_loop(0, last * pieces, sent, 0)
    for chip in range(chips):
        beside(chip).wait_send()

    def sent_last(j, carry):
        @pl.when(not_top)
        def _():
            up_last(j).wait_send()

        @pl.when(not_bottom)
        def _():
            down_last(j).wait_send()

        return carry

    lax.fori_loop(0, tail, sent_last, 0)

    def average(j, carry):
        to_mate(j).wait_recv()
        averaged[0, bit(j), :] = (0.5 * (new[bit(j), :] + theirs[bit(j), :].astype(jnp.float32))).astype(jnp.bfloat16)
        to_mate(j).wait_send()
        return carry

    lax.fori_loop(0, tail, average, 0)


def call(level, chips, factor, x, g, p, m, v, t):
    tokens, width = g.shape
    rows = p.shape[1]
    pieces, tail = PIECES, TAIL
    dma = pltpu.SemaphoreType.DMA
    any_space = pl.BlockSpec(memory_space=pl.ANY)
    return pl.pallas_call(
        functools.partial(step_kernel, level, chips, factor, pieces, tail),
        out_shape=(
            jax.ShapeDtypeStruct((tokens, width), jnp.bfloat16),
            jax.ShapeDtypeStruct((1, rows, width), jnp.bfloat16),
        ),
        in_specs=[any_space] * 5 + [pl.BlockSpec(memory_space=pltpu.SMEM)],
        out_specs=(pl.BlockSpec(memory_space=pltpu.VMEM),) * 2,
        scratch_shapes=[
            pltpu.VMEM(x.shape, jnp.bfloat16),
            pltpu.VMEM((chips, 2 * tokens, rows), jnp.bfloat16),
            pltpu.VMEM((2 * tokens, width), jnp.bfloat16),
            pltpu.VMEM((rows, width), jnp.float32),
            pltpu.VMEM((rows, width), jnp.bfloat16),
            pltpu.VMEM((rows, width), jnp.bfloat16),
            pltpu.VMEM((2 * chips, rows, width), jnp.bfloat16),
            pltpu.VMEM((chips + 1, rows, width), jnp.bfloat16),
            pltpu.VMEM((rows, width), jnp.float32),
            pltpu.VMEM((rows, width), jnp.bfloat16),
            pltpu.VMEM((rows, width), jnp.bfloat16),
            pltpu.VMEM((tokens, width), jnp.float32),
            dma((pieces,)), dma((6,)),
            dma, dma, dma, dma,
            dma(((chips - 1) * pieces + tail,)), dma(((chips - 1) * pieces + tail,)),
            dma(((chips - 1) * pieces + tail,)), dma(((chips - 1) * pieces + tail,)),
            dma((chips,)), dma((chips,)),
            dma((tail,)), dma((tail,)),
        ],
        compiler_params=pltpu.CompilerParams(
            collective_id=level, has_side_effects=True, vmem_limit_bytes=48 * 2**20
        ),
        cost_estimate=pl.CostEstimate(
            flops=4 * tokens * width * x.shape[1], bytes_accessed=6 * 2**20, transcendentals=0
        ),
        name=f"level_{level}",
    )(x, g, p, m, v, t)


def emit_kernel(first, second, first_out, second_out, sem):
    copies = [
        pltpu.make_async_copy(first, first_out, sem.at[0]),
        pltpu.make_async_copy(second, second_out, sem.at[1]),
    ]
    for copy in copies:
        copy.start()
    for copy in copies:
        copy.wait()


def emit(first, second):
    any_space = pl.BlockSpec(memory_space=pl.ANY)
    return pl.pallas_call(
        emit_kernel,
        out_shape=(
            jax.ShapeDtypeStruct(first.shape, first.dtype),
            jax.ShapeDtypeStruct(second.shape, second.dtype),
        ),
        in_specs=[any_space] * 2,
        out_specs=(any_space, any_space),
        scratch_shapes=[pltpu.SemaphoreType.DMA((2,))],
        name="emit",
    )(first, second)


def per_device(activations, key_grads, params, first_moment, second_moment, step_index):
    factor = activations.shape[1] ** (-0.5)
    chips = lax.axis_size("fsdp") // 2
    levels = lax.axis_size("rep").bit_length() - 1
    branches = [functools.partial(call, level, chips, factor) for level in range(levels)]
    key_out, averaged = lax.switch(
        lax.rem(step_index[0], levels), branches,
        activations, key_grads, params, first_moment, second_moment, step_index,
    )
    return emit(key_out, averaged)


def solution(mesh):
    in_specs = (
        P(("rep", "fsdp"), None),
        P(("rep", "fsdp"), None),
        P("rep", "fsdp", None),
        P("rep", "fsdp", None),
        P("rep", "fsdp", None),
        P(),
    )
    out_specs = (P(("rep", "fsdp"), None), P("rep", "fsdp", None))
    return jax.shard_map(
        per_device, mesh=mesh, in_specs=in_specs, out_specs=out_specs, check_vma=False
    )
```

```python
import functools
import math

import jax
import jax.numpy as jnp
from jax import lax
from jax.experimental import pallas as pl
from jax.experimental.pallas import tpu as pltpu
from jax.sharding import PartitionSpec as P

MESH = pl.DeviceIdType.MESH
beta_one = 0.9
beta_two = 0.95
learn_rate = 0.25
epsilon = 1e-08
PIECES = 2
TAIL = 8


def step_kernel(
    level, chips, factor, pieces, tail,
    x, g, p, m, v, t,
    key_out, averaged,
    xl, xc, gc, par, mom, var, wall, acc, new, mine, theirs, ksum,
    fsem, lsem, xsend, xrecv, gsend, grecv, usend, urecv, dsend, drecv, bsend, brecv, psend, precv,
):
    rep, me = lax.axis_index("rep"), lax.axis_index("fsdp")
    z = me // 2
    core = me - 2 * z
    last = chips - 1
    sib = me + 1 - 2 * core
    mask = 2**level
    mate = rep + mask * (1 - 2 * ((rep // mask) % 2))
    tokens, rows = g.shape[0], p.shape[1]
    piece, small = rows // pieces, rows // tail
    split = tail // pieces
    not_top, not_bottom = z < last, z > 0

    def block(index):
        return pl.ds(pl.multiple_of(index * rows, rows), rows)

    def part(s):
        return pl.ds(pl.multiple_of(s * piece, piece), piece)

    def bit(j):
        return pl.ds(pl.multiple_of(j * small, small), small)

    load_p = [pltpu.make_async_copy(p.at[0, part(s)], par.at[part(s)], fsem.at[s]) for s in range(pieces)]
    load_p[0].start()
    barrier = pltpu.get_barrier_semaphore()
    pl.semaphore_signal(barrier, inc=1, device_id=(mate, me), device_id_type=MESH)

    @pl.when(not_top)
    def _():
        pl.semaphore_signal(barrier, inc=1, device_id=(rep, me + 2), device_id_type=MESH)

    @pl.when(not_bottom)
    def _():
        pl.semaphore_signal(barrier, inc=1, device_id=(rep, me - 2), device_id_type=MESH)

    pl.semaphore_signal(barrier, inc=1, device_id=(rep, sib), device_id_type=MESH)

    for s in range(1, pieces):
        load_p[s].start()
    load_x = pltpu.make_async_copy(x, xl, lsem.at[1])
    load_x.start()
    load_g = pltpu.make_async_copy(g, gc.at[pl.ds(0, tokens)], lsem.at[2])
    load_g.start()
    for d in range(chips):
        pltpu.make_async_copy(
            x.at[:, block(2 * d + core)], xc.at[d, pl.ds(0, tokens)], lsem.at[3]
        ).start()
    load_m = pltpu.make_async_copy(m.at[0], mom, lsem.at[4])
    load_m.start()
    load_v = pltpu.make_async_copy(v.at[0], var, lsem.at[5])
    load_v.start()

    def up(ref, k, s):
        return pltpu.make_async_remote_copy(
            src_ref=ref, dst_ref=ref, send_sem=usend.at[k * pieces + s], recv_sem=urecv.at[k * pieces + s],
            device_id=(rep, me + 2), device_id_type=MESH,
        )

    def down(ref, k, s):
        return pltpu.make_async_remote_copy(
            src_ref=ref, dst_ref=ref, send_sem=dsend.at[k * pieces + s], recv_sem=drecv.at[k * pieces + s],
            device_id=(rep, me - 2), device_id_type=MESH,
        )

    def up_last(j):
        ref = acc.at[z + 2, bit(j)]
        return pltpu.make_async_remote_copy(
            src_ref=ref, dst_ref=ref, send_sem=usend.at[last * pieces + j], recv_sem=urecv.at[last * pieces + j],
            device_id=(rep, me + 2), device_id_type=MESH,
        )

    def down_last(j):
        ref = acc.at[z - 1, bit(j)]
        return pltpu.make_async_remote_copy(
            src_ref=ref, dst_ref=ref, send_sem=dsend.at[last * pieces + j], recv_sem=drecv.at[last * pieces + j],
            device_id=(rep, me - 2), device_id_type=MESH,
        )

    def up_from(j):
        ref = acc.at[z + 1, bit(j)]
        return pltpu.make_async_remote_copy(
            src_ref=ref, dst_ref=ref, send_sem=usend.at[last * pieces + j], recv_sem=urecv.at[last * pieces + j],
            device_id=(rep, me - 2), device_id_type=MESH,
        )

    def down_from(j):
        ref = acc.at[z, bit(j)]
        return pltpu.make_async_remote_copy(
            src_ref=ref, dst_ref=ref, send_sem=dsend.at[last * pieces + j], recv_sem=drecv.at[last * pieces + j],
            device_id=(rep, me + 2), device_id_type=MESH,
        )

    def beside(chip):
        ref = wall.at[2 * chip + core]
        return pltpu.make_async_remote_copy(
            src_ref=ref, dst_ref=ref, send_sem=bsend.at[chip], recv_sem=brecv.at[chip],
            device_id=(rep, sib), device_id_type=MESH,
        )

    def from_beside(chip):
        ref = wall.at[2 * chip + 1 - core]
        return pltpu.make_async_remote_copy(
            src_ref=ref, dst_ref=ref, send_sem=bsend.at[chip], recv_sem=brecv.at[chip],
            device_id=(rep, sib), device_id_type=MESH,
        )

    def to_mate(j):
        return pltpu.make_async_remote_copy(
            src_ref=mine.at[bit(j)], dst_ref=theirs.at[bit(j)], send_sem=psend.at[j], recv_sem=precv.at[j],
            device_id=(mate, me), device_id_type=MESH,
        )

    for s in range(pieces):
        load_p[s].wait()
        wall[me, part(s)] = par[part(s), :].astype(jnp.bfloat16)
        if s == 0:
            pl.semaphore_wait(barrier, 2 + not_top.astype(jnp.int32) + not_bottom.astype(jnp.int32))

        @pl.when(not_top)
        def _(s=s):
            up(wall.at[me, part(s)], 0, s).start()

        @pl.when(not_bottom)
        def _(s=s):
            down(wall.at[me, part(s)], 0, s).start()

    swap_g = pltpu.make_async_remote_copy(
        src_ref=g, dst_ref=gc.at[pl.ds(tokens, tokens)], send_sem=gsend, recv_sem=grecv,
        device_id=(rep, sib), device_id_type=MESH,
    )
    swap_g.start()
    for d in range(chips):
        pltpu.make_async_remote_copy(
            src_ref=x.at[:, block(2 * d + 1 - core)], dst_ref=xc.at[d, pl.ds(tokens, tokens)],
            send_sem=xsend, recv_sem=xrecv, device_id=(rep, sib), device_id_type=MESH,
        ).start()
    beside(z).start()
    load_x.wait()
    load_g.wait()
    load_m.wait()
    load_v.wait()
    whole = pltpu.make_async_remote_copy(
        src_ref=xc.at[:, pl.ds(0, tokens)], dst_ref=xc.at[:, pl.ds(tokens, tokens)],
        send_sem=xsend, recv_sem=xrecv, device_id=(rep, sib), device_id_type=MESH,
    )
    pltpu.make_async_copy(
        xc.at[:, pl.ds(0, tokens)], xc.at[:, pl.ds(0, tokens)], lsem.at[3]
    ).wait()
    whole.wait()
    swap_g.wait()

    def project(index):
        ksum[...] += jnp.dot(xl[:, block(index)], wall[index], preferred_element_type=jnp.float32)

    ksum[...] = jnp.dot(xl[:, block(me)], wall[me], preferred_element_type=jnp.float32)

    def partial(d, s):
        return lax.dot_general(
            xc[d, :, part(s)], gc[...], (((0,), (0,)), ((), ())), preferred_element_type=jnp.float32
        )

    def add_to(slot, d, s, received):
        own = partial(d, s)

        @pl.when(received)
        def _():
            acc[slot, part(s), :] = (own + acc[slot, part(s), :].astype(jnp.float32)).astype(jnp.bfloat16)

        @pl.when(jnp.logical_not(received))
        def _():
            acc[slot, part(s), :] = own.astype(jnp.bfloat16)

    def turn(i, carry):
        k, s = i // pieces, i % pieces

        @pl.when(k <= z)
        def _():
            chip = z - k
            ref = wall.at[2 * chip + core, part(s)]
            up(ref, k - 1, s).wait_recv()

            @pl.when(not_top)
            def _():
                up(ref, k, s).start()

        @pl.when(k <= last - z)
        def _():
            chip = z + k
            ref = wall.at[2 * chip + core, part(s)]
            down(ref, k - 1, s).wait_recv()

            @pl.when(not_bottom)
            def _():
                down(ref, k, s).start()

        @pl.when(k > z)
        def _():
            d = chips + z - k
            ref = acc.at[d + 1, part(s)]

            @pl.when(not_bottom)
            def _():
                up(ref, k - 1, s).wait_recv()

            add_to(d + 1, d, s, not_bottom)

            @pl.when(k < last)
            def _():
                up(ref, k, s).start()

            @pl.when(k == last)
            def _():
                for q in range(split):
                    up_last(s * split + q).start()

        @pl.when(k > last - z)
        def _():
            d = z + k - chips
            ref = acc.at[d, part(s)]

            @pl.when(not_top)
            def _():
                down(ref, k - 1, s).wait_recv()

            add_to(d, d, s, not_top)

            @pl.when(k < last)
            def _():
                down(ref, k, s).start()

            @pl.when(k == last)
            def _():
                for q in range(split):
                    down_last(s * split + q).start()

        @pl.when(s == pieces - 1)
        def _():
            @pl.when(k <= z)
            def _():
                beside(z - k).start()
                project(2 * (z - k) + core)

            @pl.when(k <= last - z)
            def _():
                beside(z + k).start()
                project(2 * (z + k) + core)

            @pl.when(k - 1 <= z)
            def _():
                from_beside(z - k + 1).wait_recv()
                project(2 * (z - k + 1) + 1 - core)

            @pl.when(jnp.logical_and(k > 1, k - 1 <= last - z))
            def _():
                from_beside(z + k - 1).wait_recv()
                project(2 * (z + k - 1) + 1 - core)

        return carry

    lax.fori_loop(pieces, chips * pieces, turn, 0)

    def own_term(s, carry):
        new[part(s), :] = partial(z, s)
        return carry

    lax.fori_loop(0, pieces, own_term, 0)

    @pl.when(z == last)
    def _():
        from_beside(0).wait_recv()
        project(1 - core)

    @pl.when(z == 0)
    def _():
        from_beside(last).wait_recv()
        project(2 * last + 1 - core)

    key_out[...] = (ksum[...] * factor).astype(jnp.bfloat16)

    steps = jnp.full((1, g.shape[1]), t[0] + 1, jnp.int32).astype(jnp.float32)
    corr_one = 1.0 - jnp.exp(steps * math.log(beta_one))
    corr_two = 1.0 - jnp.exp(steps * math.log(beta_two))

    def finish(j, carry):
        at = bit(j)
        own = new[at, :]

        @pl.when(not_bottom)
        def _():
            up_from(j).wait_recv()

        @pl.when(not_top)
        def _():
            down_from(j).wait_recv()

        below = jnp.where(not_bottom, acc[z + 1, at, :].astype(jnp.float32), 0.0)
        above = jnp.where(not_top, acc[z, at, :].astype(jnp.float32), 0.0)
        gradient = (own + below + above) * factor
        one = beta_one * mom[at, :].astype(jnp.float32) + (1.0 - beta_one) * gradient
        two = beta_two * var[at, :].astype(jnp.float32) + (1.0 - beta_two) * gradient * gradient
        updated = par[at, :] - learn_rate * (one / corr_one) / (jnp.sqrt(two / corr_two) + epsilon)
        new[at, :] = updated
        mine[at, :] = updated.astype(jnp.bfloat16)
        to_mate(j).start()
        return carry

    lax.fori_loop(0, tail, finish, 0)

    def sent(i, carry):
        k, s = i // pieces, i % pieces

        @pl.when(not_top)
        def _():
            up(acc.at[0, part(s)], k, s).wait_send()

        @pl.when(not_bottom)
        def _():
            down(acc.at[0, part(s)], k, s).wait_send()

        return carry

    lax.fori_loop(0, last * pieces, sent, 0)
    for chip in range(chips):
        beside(chip).wait_send()

    def sent_last(j, carry):
        @pl.when(not_top)
        def _():
            up_last(j).wait_send()

        @pl.when(not_bottom)
        def _():
            down_last(j).wait_send()

        return carry

    lax.fori_loop(0, tail, sent_last, 0)

    def average(j, carry):
        to_mate(j).wait_recv()
        averaged[0, bit(j), :] = (0.5 * (new[bit(j), :] + theirs[bit(j), :].astype(jnp.float32))).astype(jnp.bfloat16)
        to_mate(j).wait_send()
        return carry

    lax.fori_loop(0, tail, average, 0)


def call(level, chips, factor, x, g, p, m, v, t):
    tokens, width = g.shape
    rows = p.shape[1]
    pieces, tail = PIECES, TAIL if level % 2 else TAIL // 2
    dma = pltpu.SemaphoreType.DMA
    any_space = pl.BlockSpec(memory_space=pl.ANY)
    return pl.pallas_call(
        functools.partial(step_kernel, level, chips, factor, pieces, tail),
        out_shape=(
            jax.ShapeDtypeStruct((tokens, width), jnp.bfloat16),
            jax.ShapeDtypeStruct((1, rows, width), jnp.bfloat16),
        ),
        in_specs=[any_space] * 5 + [pl.BlockSpec(memory_space=pltpu.SMEM)],
        out_specs=(pl.BlockSpec(memory_space=pltpu.VMEM),) * 2,
        scratch_shapes=[
            pltpu.VMEM(x.shape, jnp.bfloat16),
            pltpu.VMEM((chips, 2 * tokens, rows), jnp.bfloat16),
            pltpu.VMEM((2 * tokens, width), jnp.bfloat16),
            pltpu.VMEM((rows, width), jnp.float32),
            pltpu.VMEM((rows, width), jnp.bfloat16),
            pltpu.VMEM((rows, width), jnp.bfloat16),
            pltpu.VMEM((2 * chips, rows, width), jnp.bfloat16),
            pltpu.VMEM((chips + 1, rows, width), jnp.bfloat16),
            pltpu.VMEM((rows, width), jnp.float32),
            pltpu.VMEM((rows, width), jnp.bfloat16),
            pltpu.VMEM((rows, width), jnp.bfloat16),
            pltpu.VMEM((tokens, width), jnp.float32),
            dma((pieces,)), dma((6,)),
            dma, dma, dma, dma,
            dma(((chips - 1) * pieces + tail,)), dma(((chips - 1) * pieces + tail,)),
            dma(((chips - 1) * pieces + tail,)), dma(((chips - 1) * pieces + tail,)),
            dma((chips,)), dma((chips,)),
            dma((tail,)), dma((tail,)),
        ],
        compiler_params=pltpu.CompilerParams(
            collective_id=level, has_side_effects=True, vmem_limit_bytes=48 * 2**20
        ),
        cost_estimate=pl.CostEstimate(
            flops=4 * tokens * width * x.shape[1], bytes_accessed=6 * 2**20, transcendentals=0
        ),
        name=f"level_{level}",
    )(x, g, p, m, v, t)


def emit_kernel(first, second, first_out, second_out, sem):
    copies = [
        pltpu.make_async_copy(first, first_out, sem.at[0]),
        pltpu.make_async_copy(second, second_out, sem.at[1]),
    ]
    for copy in copies:
        copy.start()
    for copy in copies:
        copy.wait()


def emit(first, second):
    any_space = pl.BlockSpec(memory_space=pl.ANY)
    return pl.pallas_call(
        emit_kernel,
        out_shape=(
            jax.ShapeDtypeStruct(first.shape, first.dtype),
            jax.ShapeDtypeStruct(second.shape, second.dtype),
        ),
        in_specs=[any_space] * 2,
        out_specs=(any_space, any_space),
        scratch_shapes=[pltpu.SemaphoreType.DMA((2,))],
        name="emit",
    )(first, second)


def per_device(activations, key_grads, params, first_moment, second_moment, step_index):
    factor = activations.shape[1] ** (-0.5)
    chips = lax.axis_size("fsdp") // 2
    levels = lax.axis_size("rep").bit_length() - 1
    branches = [functools.partial(call, level, chips, factor) for level in range(levels)]
    key_out, averaged = lax.switch(
        lax.rem(step_index[0], levels), branches,
        activations, key_grads, params, first_moment, second_moment, step_index,
    )
    return emit(key_out, averaged)


def solution(mesh):
    in_specs = (
        P(("rep", "fsdp"), None),
        P(("rep", "fsdp"), None),
        P("rep", "fsdp", None),
        P("rep", "fsdp", None),
        P("rep", "fsdp", None),
        P(),
    )
    out_specs = (P(("rep", "fsdp"), None), P("rep", "fsdp", None))
    return jax.shard_map(
        per_device, mesh=mesh, in_specs=in_specs, out_specs=out_specs, check_vma=False
    )
```
